512 devices in a mesh: slab: 32 (over y_lo, x, core), filt: 16 (over y_hi, z).
Axes of the slice: x: 4, y: 8 (y_hi: 2, y_lo: 4; y = y_hi * 4 + y_lo), z: 8, core: 2. Of those that a mesh axis runs over, the one named last changes fastest.
Arguments:
- volume: bfloat16 [512, 32, 1024], P('filt', 'slab'), may hold values from -6 to 6
- kernel: bfloat16 [27, 512, 512], P(None, 'filt'), may hold values from -0.0546875 to 0.0546875
- channel_bias: float32 [512], P('filt'), may hold values from -3 to 3
Outputs:
- feature_out: bfloat16 [512, 32, 1024], P('filt', 'slab')
The draws below stay inside these ranges and needn't reach their ends.
All inputs are finite; a program needn't handle non-finite values.
Results may differ from the reference program's by a relative error of at most 0.001.
Values may be sent and summed in bfloat16 or wider, within the bound.
No kernel may reach another device: no remote copies, remote signals or barrier semaphores. Data moves between devices by JAX's collectives and lax.ppermute only.
A program may use at most 128 MiB of HBM per device.

```python
import jax
import jax.numpy as jnp
from jax import lax

CIN = 512
COUT = 512
SIDE = 32
NZ = 32


def levels(key, dims, pieces, least, high):
    gain = 1.0
    for position, shards_of in pieces:
        draws = jax.random.uniform(jax.random.fold_in(jax.random.fold_in(key, 6), position), (shards_of,), jnp.float32, least / len(pieces), high / len(pieces))
        gain = gain * jnp.repeat(jnp.exp(draws), dims[position] // shards_of).reshape((-1,) + (1,) * (len(dims) - 1 - position))
    return gain


def gaussian(stream_key, extent, width, bound, split=(), held_as=jnp.bfloat16):
    array = width * jax.random.normal(stream_key, extent, jnp.float32)
    if split:
        array = array * levels(stream_key, extent, split, -0.22, 0.18)
    return jnp.clip(array, -bound, bound).astype(held_as)


def setup_inputs(seed: int = 0) -> dict:
    key_of = jax.random.split(jax.random.key(seed), 4)
    return {
        "volume": gaussian(key_of[0], (CIN, NZ, SIDE * SIDE), 1.0, 6.0, ((0, 16), (1, 32))),
        "kernel": gaussian(key_of[1], (27, COUT, CIN), (27 * CIN) ** -0.5, 0.0546875, ((1, 16),)),
        "channel_bias": gaussian(key_of[2], (COUT,), 0.5, 3.0, ((0, 16),), jnp.float32),
    }


def reference(volume, kernel, channel_bias):
    framed = volume.astype(jnp.float32).reshape(CIN, NZ, SIDE, SIDE)
    framed = jnp.pad(framed, ((0, 0), (1, 1), (1, 1), (1, 1)))
    running = jnp.zeros((COUT, NZ * SIDE * SIDE), jnp.float32)
    for tap_index in range(27):
        plane_off = tap_index // 9
        row_off = (tap_index // 3) % 3
        col_off = tap_index % 3
        shifted = framed[:, plane_off:plane_off + NZ, row_off:row_off + SIDE, col_off:col_off + SIDE]
        shifted = shifted.reshape(CIN, NZ * SIDE * SIDE)
        weights_tap = kernel[tap_index].astype(jnp.float32)
        running = running + jnp.dot(weights_tap, shifted, preferred_element_type=jnp.float32, precision=lax.Precision.HIGHEST)
    running = running + channel_bias[:, None]
    return running.reshape(COUT, NZ, SIDE * SIDE).astype(jnp.bfloat16)
```

```python
import jax
import jax.numpy as jnp
from jax import lax
from jax.experimental import pallas as pl
from jax.experimental.pallas import tpu as pltpu
from jax.sharding import PartitionSpec as P

SIDE = 32


def shifted_rows(value, rows):
    cells = value.shape[1]
    place = lax.broadcasted_iota(jnp.int32, value.shape, 1)
    moved = pltpu.roll(value, (rows * SIDE) % cells, 1)
    inside = place >= rows * SIDE if rows > 0 else place < cells + rows * SIDE
    return jnp.where(inside, moved, 0.0)


def shifted_cols(value, cols):
    cells = value.shape[1]
    column = lax.broadcasted_iota(jnp.int32, value.shape, 1) % SIDE
    moved = pltpu.roll(value, cols % cells, 1)
    inside = column >= 1 if cols > 0 else column <= SIDE - 2
    return jnp.where(inside, moved, 0.0)


def taps_kernel(parity_ref, plane_ref, weight_ref, bias_ref, centre_ref, pair_ref, next_ref):
    out_rows = weight_ref.shape[1]
    plane = plane_ref[...]
    sums = []
    for plane_off in range(3):
        group = weight_ref[9 * plane_off : 9 * plane_off + 9].reshape(
            9 * out_rows, weight_ref.shape[2]
        )
        product = jnp.dot(group, plane, preferred_element_type=jnp.float32)
        taps = [
            product[tap * out_rows : (tap + 1) * out_rows] for tap in range(9)
        ]
        by_col = [
            taps[3 + col] + shifted_rows(taps[col], 1) + shifted_rows(taps[6 + col], -1)
            for col in range(3)
        ]
        sums.append(
            by_col[1] + shifted_cols(by_col[0], 1) + shifted_cols(by_col[2], -1)
        )
    above, own, below = sums
    even = parity_ref[0] == 0
    centre_ref[...] = own + bias_ref[...]
    pair_ref[...] = jnp.where(even, above, below)
    next_ref[...] = jnp.where(even, below, above)


def taps(parity, plane, weights, bias):
    out_rows = weights.shape[1]
    cells = plane.shape[1]
    out = jax.ShapeDtypeStruct((out_rows, cells), jnp.float32)
    vmem = pl.BlockSpec(memory_space=pltpu.VMEM)
    return pl.pallas_call(
        taps_kernel,
        out_shape=(out, out, out),
        in_specs=[pl.BlockSpec(memory_space=pltpu.SMEM), vmem, vmem, vmem],
        out_specs=(vmem, vmem, vmem),
        compiler_params=pltpu.CompilerParams(vmem_limit_bytes=40 * 1024 * 1024),
    )(parity, plane, weights, bias)


def on_device(volume, kernel, channel_bias):
    own_in, planes, cells = volume.shape
    own_out = kernel.shape[1]
    filt = lax.axis_size("filt")
    slabs = lax.axis_size("slab")
    copies = jnp.broadcast_to(volume.reshape(1, own_in, cells), (filt, own_in, cells))
    gathered = lax.all_to_all(copies, "filt", 0, 0)
    plane = gathered.reshape(filt * own_in, cells)
    parity = (lax.axis_index("slab") % 2).reshape(1)
    centre, to_pair, to_next = taps(parity, plane, kernel, channel_bias[:, None])
    pairs = [(i, i ^ 1) for i in range(slabs)]
    nexts = [(i, i + 1) for i in range(1, slabs - 1, 2)]
    nexts += [(target, source) for source, target in nexts]
    from_next = lax.ppermute(to_next, "slab", nexts)
    from_pair = lax.ppermute(to_pair, "slab", pairs)
    summed = centre + from_pair + from_next
    return summed.reshape(own_out, planes, cells).astype(jnp.bfloat16)


def solution(mesh):
    return jax.shard_map(
        on_device,
        mesh=mesh,
        in_specs=(P("filt", "slab", None), P(None, "filt", None), P("filt")),
        out_specs=P("filt", "slab", None),
        check_vma=False,
    )
```

```python
import jax
import jax.numpy as jnp
from jax import lax
from jax.experimental import pallas as pl
from jax.experimental.pallas import tpu as pltpu
from jax.sharding import PartitionSpec as P

SIDE = 32


def shifted_rows(value, rows):
    cells = value.shape[1]
    place = lax.broadcasted_iota(jnp.int32, value.shape, 1)
    moved = pltpu.roll(value, (rows * SIDE) % cells, 1)
    inside = place >= rows * SIDE if rows > 0 else place < cells + rows * SIDE
    return jnp.where(inside, moved, 0.0)


def shifted_cols(value, cols):
    cells = value.shape[1]
    column = lax.broadcasted_iota(jnp.int32, value.shape, 1) % SIDE
    moved = pltpu.roll(value, cols % cells, 1)
    inside = column >= 1 if cols > 0 else column <= SIDE - 2
    return jnp.where(inside, moved, 0.0)


def plane_taps(plane, weight_ref, plane_off):
    out_rows, channels = weight_ref.shape[1:]
    group = weight_ref[pl.ds(9 * plane_off, 9)].reshape(9 * out_rows, channels)
    product = jnp.dot(group, plane, preferred_element_type=jnp.float32)
    taps = [product[tap * out_rows : (tap + 1) * out_rows] for tap in range(9)]
    by_col = [
        taps[3 + col] + shifted_rows(taps[col], 1) + shifted_rows(taps[6 + col], -1)
        for col in range(3)
    ]
    return by_col[1] + shifted_cols(by_col[0], 1) + shifted_cols(by_col[2], -1)


def next_kernel(odd_ref, plane_ref, weight_ref, next_ref):
    next_ref[...] = plane_taps(plane_ref[...], weight_ref, 2 - 2 * odd_ref[0])


def rest_kernel(odd_ref, plane_ref, weight_ref, pair_ref, centre_ref):
    plane = plane_ref[...]
    pair_ref[...] = plane_taps(plane, weight_ref, 2 * odd_ref[0])
    centre_ref[...] = plane_taps(plane, weight_ref, 1)


def copies_kernel(block_ref, copies_ref):
    block = block_ref[...]
    for i in range(copies_ref.shape[0]):
        copies_ref[i] = block


VMEM = pl.BlockSpec(memory_space=pltpu.VMEM)
SMEM = pl.BlockSpec(memory_space=pltpu.SMEM)
PARAMS = pltpu.CompilerParams(vmem_limit_bytes=40 * 1024 * 1024)


def add_kernel(first_ref, second_ref, out_ref):
    out_ref[...] = first_ref[...] + second_ref[...]


def added(first, second):
    return pl.pallas_call(
        add_kernel,
        out_shape=jax.ShapeDtypeStruct(first.shape, first.dtype),
        in_specs=[VMEM, VMEM],
        out_specs=VMEM,
        compiler_params=PARAMS,
        cost_estimate=pl.CostEstimate(flops=10**10, bytes_accessed=0, transcendentals=0),
    )(first, second)


def taps(body, outs, odd, plane, weights):
    out = jax.ShapeDtypeStruct((weights.shape[1], plane.shape[1]), jnp.float32)
    return pl.pallas_call(
        body,
        out_shape=(out,) * outs,
        in_specs=[SMEM, VMEM, VMEM],
        out_specs=(VMEM,) * outs,
        compiler_params=PARAMS,
    )(odd, plane, weights)


def copied(block, count):
    return pl.pallas_call(
        copies_kernel,
        out_shape=jax.ShapeDtypeStruct((count,) + block.shape, block.dtype),
        in_specs=[VMEM],
        out_specs=VMEM,
        compiler_params=PARAMS,
    )(block)


def on_device(volume, kernel, channel_bias):
    own_in, planes, cells = volume.shape
    own_out = kernel.shape[1]
    filt = lax.axis_size("filt")
    slabs = lax.axis_size("slab")
    copies = copied(volume.reshape(own_in, cells), filt)
    gathered = lax.all_to_all(copies, "filt", 0, 0)
    plane = gathered.reshape(filt * own_in, cells)
    odd = (lax.axis_index("slab") % 2).astype(jnp.int32).reshape(1)
    pairs = [(i, i ^ 1) for i in range(slabs)]
    nexts = [(i, i + 1) for i in range(1, slabs - 1, 2)]
    nexts += [(target, source) for source, target in nexts]
    (to_next,) = taps(next_kernel, 1, odd, plane, kernel)
    from_next = lax.ppermute(to_next, "slab", nexts)
    to_pair, centre = taps(rest_kernel, 2, odd, plane, kernel)
    from_pair = lax.ppermute(to_pair, "slab", pairs)
    summed = added(centre, from_next) + from_pair + channel_bias[:, None]
    return summed.reshape(own_out, planes, cells).astype(jnp.bfloat16)


def solution(mesh):
    return jax.shard_map(
        on_device,
        mesh=mesh,
        in_specs=(P("filt", "slab", None), P(None, "filt", None), P("filt")),
        out_specs=P("filt", "slab", None),
        check_vma=False,
    )
```

```python
import functools

import jax
import jax.numpy as jnp
from jax import lax
from jax.experimental import pallas as pl
from jax.experimental.pallas import tpu as pltpu
from jax.sharding import PartitionSpec as P

SIDE = 32


def shifted_rows(value, rows):
    cells = value.shape[1]
    place = lax.broadcasted_iota(jnp.int32, value.shape, 1)
    moved = pltpu.roll(value, (rows * SIDE) % cells, 1)
    inside = place >= rows * SIDE if rows > 0 else place < cells + rows * SIDE
    return jnp.where(inside, moved, 0.0)


def shifted_cols(value, cols):
    cells = value.shape[1]
    column = lax.broadcasted_iota(jnp.int32, value.shape, 1) % SIDE
    moved = pltpu.roll(value, cols % cells, 1)
    inside = column >= 1 if cols > 0 else column <= SIDE - 2
    return jnp.where(inside, moved, 0.0)


VMEM = pl.BlockSpec(memory_space=pltpu.VMEM)
SMEM = pl.BlockSpec(memory_space=pltpu.SMEM)
PARAMS = pltpu.CompilerParams(vmem_limit_bytes=40 * 1024 * 1024)


def pick_kernel(block, place_ref, weight_ref, own_ref, send_ref):
    taps, out_rows, channels = weight_ref.shape
    rows = weight_ref[...].reshape(taps * out_rows, channels)
    shape = (channels, channels // 2)
    source = lax.broadcasted_iota(jnp.int32, shape, 0)
    target = lax.broadcasted_iota(jnp.int32, shape, 1)
    side = target // block % 2
    member = target // (2 * block)
    base = side * (channels // 2) + 2 * member * block + target % block
    for ref, parity in ((send_ref, 1 - place_ref[1]), (own_ref, place_ref[1])):
        matrix = jnp.where(source == base + parity * block, 1.0, 0.0).astype(jnp.bfloat16)
        picked = jnp.dot(rows, matrix, preferred_element_type=jnp.float32)
        ref[...] = picked.astype(jnp.bfloat16)


def picked(block, place, weights):
    taps, out_rows, channels = weights.shape
    out = jax.ShapeDtypeStruct((taps * out_rows, channels // 2), weights.dtype)
    return pl.pallas_call(
        functools.partial(pick_kernel, block),
        out_shape=(out, out),
        in_specs=[SMEM, VMEM],
        out_specs=(VMEM, VMEM),
        compiler_params=PARAMS,
    )(place, weights)


def add_kernel(first_ref, second_ref, out_ref):
    out_ref[...] = first_ref[...] + second_ref[...]


def added(first, second):
    return pl.pallas_call(
        add_kernel,
        out_shape=jax.ShapeDtypeStruct(first.shape, first.dtype),
        in_specs=[VMEM, VMEM],
        out_specs=VMEM,
        compiler_params=PARAMS,
        cost_estimate=pl.CostEstimate(flops=10**10, bytes_accessed=0, transcendentals=0),
    )(first, second)


def in_plane(product):
    rows = product.shape[0] // 9
    taps = [product[tap * rows : (tap + 1) * rows] for tap in range(9)]
    by_col = [
        taps[3 + col] + shifted_rows(taps[col], 1) + shifted_rows(taps[6 + col], -1)
        for col in range(3)
    ]
    return by_col[1] + shifted_cols(by_col[0], 1) + shifted_cols(by_col[2], -1)


def plane_taps(plane, weight_ref, plane_off):
    rows = weight_ref.shape[0] // 3
    group = weight_ref[pl.ds(plane_off * rows, rows), :]
    return in_plane(jnp.dot(group, plane, preferred_element_type=jnp.float32))


def next_kernel(place_ref, plane_ref, own_ref, other_ref, next_ref):
    plane = plane_ref[...]
    away = 2 - 2 * place_ref[0]
    out_rows = next_ref.shape[0] // 2
    next_ref[:out_rows] = plane_taps(plane, own_ref, away)
    next_ref[out_rows:] = plane_taps(plane, other_ref, away)


def rest_kernel(place_ref, plane_ref, own_ref, other_ref, pair_ref, centre_ref):
    plane = plane_ref[...]
    out_rows = pair_ref.shape[0] // 2
    for ref, off in ((pair_ref, 2 * place_ref[0]), (centre_ref, 1)):
        ref[:out_rows] = plane_taps(plane, own_ref, off)
        ref[out_rows:] = plane_taps(plane, other_ref, off)


def taps(body, outs, place, plane, own, other):
    out_rows = 2 * own.shape[0] // 27
    out = jax.ShapeDtypeStruct((out_rows, plane.shape[1]), jnp.float32)
    return pl.pallas_call(
        body,
        out_shape=(out,) * outs,
        in_specs=[SMEM] + [VMEM] * 3,
        out_specs=(VMEM,) * outs,
        compiler_params=PARAMS,
    )(place, plane, own, other)


def on_device(volume, kernel, channel_bias):
    own_in, planes, cells = volume.shape
    own_out = kernel.shape[1]
    filt = lax.axis_size("filt")
    slabs = lax.axis_size("slab")
    ring = filt // 2
    rings = [[i, i + ring] for i in range(ring)]
    partners = [(i, i ^ 1) for i in range(filt)]
    alike = [
        list(range(half * ring + parity, (half + 1) * ring, 2))
        for half in range(2)
        for parity in range(2)
    ]
    pairs = [(i, i ^ 1) for i in range(slabs)]
    nexts = [(i, i + 1) for i in range(1, slabs - 1, 2)]
    nexts += [(target, source) for source, target in nexts]
    place = jnp.stack([lax.axis_index("slab") % 2, lax.axis_index("filt") % 2])
    place = place.astype(jnp.int32)

    own, for_partner = picked(own_in, place, kernel)
    other = lax.ppermute(for_partner, "filt", partners)
    block = volume.reshape(own_in, cells)
    both = lax.all_gather(block, "filt", axis=0, tiled=True, axis_index_groups=rings)
    plane = lax.all_gather(both, "filt", axis=0, tiled=True, axis_index_groups=alike)

    (to_next,) = taps(next_kernel, 1, place, plane, own, other)
    from_next = lax.ppermute(to_next, "slab", nexts)
    to_pair, centre = taps(rest_kernel, 2, place, plane, own, other)
    from_pair = lax.ppermute(to_pair, "slab", pairs)
    centre = added(centre, from_next)
    from_other = lax.ppermute(centre[own_out:] + from_pair[own_out:], "filt", partners)
    summed = centre[:own_out] + from_pair[:own_out] + from_other + channel_bias[:, None]
    return summed.reshape(own_out, planes, cells).astype(jnp.bfloat16)


def solution(mesh):
    return jax.shard_map(
        on_device,
        mesh=mesh,
        in_specs=(P("filt", "slab", None), P(None, "filt", None), P("filt")),
        out_specs=P("filt", "slab", None),
        check_vma=False,
    )
```

```python
import functools

import jax
import jax.numpy as jnp
from jax import lax
from jax.experimental import pallas as pl
from jax.experimental.pallas import tpu as pltpu
from jax.sharding import PartitionSpec as P

SIDE = 32


def shifted_rows(value, rows):
    cells = value.shape[1]
    place = lax.broadcasted_iota(jnp.int32, value.shape, 1)
    moved = pltpu.roll(value, (rows * SIDE) % cells, 1)
    inside = place >= rows * SIDE if rows > 0 else place < cells + rows * SIDE
    return jnp.where(inside, moved, 0.0)


def shifted_cols(value, cols):
    cells = value.shape[1]
    column = lax.broadcasted_iota(jnp.int32, value.shape, 1) % SIDE
    moved = pltpu.roll(value, cols % cells, 1)
    inside = column >= 1 if cols > 0 else column <= SIDE - 2
    return jnp.where(inside, moved, 0.0)


VMEM = pl.BlockSpec(memory_space=pltpu.VMEM)
SMEM = pl.BlockSpec(memory_space=pltpu.SMEM)
PARAMS = pltpu.CompilerParams(vmem_limit_bytes=40 * 1024 * 1024)


def add_kernel(first_ref, second_ref, out_ref):
    out_ref[...] = first_ref[...] + second_ref[...]


def added(first, second):
    return pl.pallas_call(
        add_kernel,
        out_shape=jax.ShapeDtypeStruct(first.shape, first.dtype),
        in_specs=[VMEM, VMEM],
        out_specs=VMEM,
        compiler_params=PARAMS,
        cost_estimate=pl.CostEstimate(flops=10**10, bytes_accessed=0, transcendentals=0),
    )(first, second)


def in_plane(product):
    rows = product.shape[0] // 9
    taps = [product[tap * rows : (tap + 1) * rows] for tap in range(9)]
    by_col = [
        taps[3 + col] + shifted_rows(taps[col], 1) + shifted_rows(taps[6 + col], -1)
        for col in range(3)
    ]
    return by_col[1] + shifted_cols(by_col[0], 1) + shifted_cols(by_col[2], -1)


def plane_taps(plane, weight_ref, plane_off):
    out_rows, channels = weight_ref.shape[1:]
    group = weight_ref[pl.ds(9 * plane_off, 9)].reshape(9 * out_rows, channels)
    return in_plane(jnp.dot(group, plane, preferred_element_type=jnp.float32))


def next_kernel(block, place_ref, own_ref, low_ref, high_ref, weight_ref, next_ref, plane_ref):
    parity = place_ref[1]
    sides = 2
    members = own_ref.shape[0] // (sides * block)
    for member in range(members):
        for side in range(sides):
            row = (sides * member + side) * block
            for ref, first, at in (
                (own_ref, row, parity),
                (low_ref, row, 1 - parity),
                (high_ref, row - low_ref.shape[0], 1 - parity),
            ):
                if 0 <= first < ref.shape[0]:
                    target = (side * 2 * members + 2 * member + at) * block
                    plane_ref[pl.ds(pl.multiple_of(target, block), block)] = ref[
                        first : first + block
                    ]
    next_ref[...] = plane_taps(plane_ref[...], weight_ref, 2 - 2 * place_ref[0])


def rest_kernel(place_ref, plane_ref, weight_ref, pair_ref, centre_ref):
    plane = plane_ref[...]
    pair_ref[...] = plane_taps(plane, weight_ref, 2 * place_ref[0])
    centre_ref[...] = plane_taps(plane, weight_ref, 1)


def called(body, out_shape, *args):
    return pl.pallas_call(
        body,
        out_shape=out_shape,
        in_specs=[SMEM] + [VMEM] * (len(args) - 1),
        out_specs=(VMEM,) * len(out_shape),
        compiler_params=PARAMS,
    )(*args)


def on_device(volume, kernel, channel_bias):
    own_in, planes, cells = volume.shape
    own_out = kernel.shape[1]
    filt = lax.axis_size("filt")
    slabs = lax.axis_size("slab")
    ring = filt // 2
    rings = [[i, i + ring] for i in range(ring)]
    alike = [
        list(range(half * ring + parity, (half + 1) * ring, 2))
        for half in range(2)
        for parity in range(2)
    ]
    down = [(i, i // ring * ring + (i - 1) % ring) for i in range(filt)]
    up = [(target, source) for source, target in down]
    pairs = [(i, i ^ 1) for i in range(slabs)]
    nexts = [(i, i + 1) for i in range(1, slabs - 1, 2)]
    nexts += [(target, source) for source, target in nexts]
    place = jnp.stack([lax.axis_index("slab") % 2, lax.axis_index("filt") % 2])
    place = place.astype(jnp.int32)

    block = volume.reshape(own_in, cells)
    both = lax.all_gather(block, "filt", axis=0, tiled=True, axis_index_groups=rings)
    own = lax.all_gather(both, "filt", axis=0, tiled=True, axis_index_groups=alike)
    half = own.shape[0] // 2
    low = lax.ppermute(own[:half], "filt", down)
    high = lax.ppermute(own[half:], "filt", up)

    part = jax.ShapeDtypeStruct((own_out, cells), jnp.float32)
    whole = jax.ShapeDtypeStruct((filt * own_in, cells), volume.dtype)
    to_next, plane = called(
        functools.partial(next_kernel, own_in), (part, whole), place, own, low, high, kernel
    )
    from_next = lax.ppermute(to_next, "slab", nexts)
    to_pair, centre = called(rest_kernel, (part, part), place, plane, kernel)
    from_pair = lax.ppermute(to_pair, "slab", pairs)
    summed = added(centre, from_next) + from_pair + channel_bias[:, None]
    return summed.reshape(own_out, planes, cells).astype(jnp.bfloat16)


def solution(mesh):
    return jax.shard_map(
        on_device,
        mesh=mesh,
        in_specs=(P("filt", "slab", None), P(None, "filt", None), P("filt")),
        out_specs=P("filt", "slab", None),
        check_vma=False,
    )
```

```python
import functools

import jax
import jax.numpy as jnp
from jax import lax
from jax.experimental import pallas as pl
from jax.experimental.pallas import tpu as pltpu
from jax.sharding import PartitionSpec as P

SIDE = 32


def shifted_rows(value, rows):
    cells = value.shape[1]
    place = lax.broadcasted_iota(jnp.int32, value.shape, 1)
    moved = pltpu.roll(value, (rows * SIDE) % cells, 1)
    inside = place >= rows * SIDE if rows > 0 else place < cells + rows * SIDE
    return jnp.where(inside, moved, 0.0)


def shifted_cols(value, cols):
    cells = value.shape[1]
    column = lax.broadcasted_iota(jnp.int32, value.shape, 1) % SIDE
    moved = pltpu.roll(value, cols % cells, 1)
    inside = column >= 1 if cols > 0 else column <= SIDE - 2
    return jnp.where(inside, moved, 0.0)


VMEM = pl.BlockSpec(memory_space=pltpu.VMEM)
SMEM = pl.BlockSpec(memory_space=pltpu.SMEM)
PARAMS = pltpu.CompilerParams(vmem_limit_bytes=40 * 1024 * 1024)


def add_kernel(first_ref, second_ref, out_ref):
    out_ref[...] = first_ref[...] + second_ref[...]


def added(first, second):
    return pl.pallas_call(
        add_kernel,
        out_shape=jax.ShapeDtypeStruct(first.shape, first.dtype),
        in_specs=[VMEM, VMEM],
        out_specs=VMEM,
        compiler_params=PARAMS,
        cost_estimate=pl.CostEstimate(flops=10**10, bytes_accessed=0, transcendentals=0),
    )(first, second)


def in_plane(product):
    rows = product.shape[0] // 9
    taps = [product[tap * rows : (tap + 1) * rows] for tap in range(9)]
    by_col = [
        taps[3 + col] + shifted_rows(taps[col], 1) + shifted_rows(taps[6 + col], -1)
        for col in range(3)
    ]
    return by_col[1] + shifted_cols(by_col[0], 1) + shifted_cols(by_col[2], -1)


def plane_taps(plane, weight_ref, plane_off):
    out_rows, channels = weight_ref.shape[1:]
    group = weight_ref[pl.ds(9 * plane_off, 9)].reshape(9 * out_rows, channels)
    return in_plane(jnp.dot(group, plane, preferred_element_type=jnp.float32))


def in_order(block, parity, own_ref, low_ref, high_ref, plane_ref):
    sides = 2
    members = own_ref.shape[0] // (sides * block)
    for member in range(members):
        for side in range(sides):
            row = (sides * member + side) * block
            for ref, first, at in (
                (own_ref, row, parity),
                (low_ref, row, 1 - parity),
                (high_ref, row - low_ref.shape[0], 1 - parity),
            ):
                if 0 <= first < ref.shape[0]:
                    target = (side * 2 * members + 2 * member + at) * block
                    plane_ref[pl.ds(pl.multiple_of(target, block), block)] = ref[
                        first : first + block
                    ]


def away_kernel(
    block, place_ref, own_ref, low_ref, high_ref, weight_ref, next_ref, pair_ref, plane_ref
):
    in_order(block, place_ref[1], own_ref, low_ref, high_ref, plane_ref)
    plane = plane_ref[...]
    next_ref[...] = plane_taps(plane, weight_ref, 2 - 2 * place_ref[0])
    pair_ref[...] = plane_taps(plane, weight_ref, 2 * place_ref[0])


def centre_kernel(
    block, place_ref, own_ref, low_ref, high_ref, weight_ref, centre_ref, plane_ref
):
    in_order(block, place_ref[1], own_ref, low_ref, high_ref, plane_ref)
    centre_ref[...] = plane_taps(plane_ref[...], weight_ref, 1)


def called(body, out_shape, scratch, *args):
    return pl.pallas_call(
        body,
        out_shape=out_shape,
        in_specs=[SMEM] + [VMEM] * (len(args) - 1),
        out_specs=(VMEM,) * len(out_shape),
        scratch_shapes=[scratch],
        compiler_params=PARAMS,
    )(*args)


def on_device(volume, kernel, channel_bias):
    own_in, planes, cells = volume.shape
    own_out = kernel.shape[1]
    filt = lax.axis_size("filt")
    slabs = lax.axis_size("slab")
    ring = filt // 2
    rings = [[i, i + ring] for i in range(ring)]
    alike = [
        list(range(half * ring + parity, (half + 1) * ring, 2))
        for half in range(2)
        for parity in range(2)
    ]
    down = [(i, i // ring * ring + (i - 1) % ring) for i in range(filt)]
    up = [(target, source) for source, target in down]
    pairs = [(i, i ^ 1) for i in range(slabs)]
    nexts = [(i, i + 1) for i in range(1, slabs - 1, 2)]
    nexts += [(target, source) for source, target in nexts]
    place = jnp.stack([lax.axis_index("slab") % 2, lax.axis_index("filt") % 2])
    place = place.astype(jnp.int32)

    block = volume.reshape(own_in, cells)
    both = lax.all_gather(block, "filt", axis=0, tiled=True, axis_index_groups=rings)
    own = lax.all_gather(both, "filt", axis=0, tiled=True, axis_index_groups=alike)
    half = own.shape[0] // 2
    low = lax.ppermute(own[:half], "filt", down)
    high = lax.ppermute(own[half:], "filt", up)

    part = jax.ShapeDtypeStruct((own_out, cells), jnp.float32)
    scratch = pltpu.VMEM((filt * own_in, cells), volume.dtype)
    gathered = (place, own, low, high, kernel)
    to_next, to_pair = called(
        functools.partial(away_kernel, own_in), (part, part), scratch, *gathered
    )
    from_next = lax.ppermute(to_next, "slab", nexts)
    from_pair = lax.ppermute(to_pair, "slab", pairs)
    (centre,) = called(functools.partial(centre_kernel, own_in), (part,), scratch, *gathered)
    summed = added(centre, from_next) + from_pair + channel_bias[:, None]
    return summed.reshape(own_out, planes, cells).astype(jnp.bfloat16)


def solution(mesh):
    return jax.shard_map(
        on_device,
        mesh=mesh,
        in_specs=(P("filt", "slab", None), P(None, "filt", None), P("filt")),
        out_specs=P("filt", "slab", None),
        check_vma=False,
    )
```

```python
import functools

import jax
import jax.numpy as jnp
from jax import lax
from jax.experimental import pallas as pl
from jax.experimental.pallas import tpu as pltpu
from jax.sharding import PartitionSpec as P

SIDE = 32


def shifted_rows(value, rows):
    cells = value.shape[1]
    place = lax.broadcasted_iota(jnp.int32, value.shape, 1)
    moved = pltpu.roll(value, (rows * SIDE) % cells, 1)
    inside = place >= rows * SIDE if rows > 0 else place < cells + rows * SIDE
    return jnp.where(inside, moved, 0.0)


def shifted_cols(value, cols):
    cells = value.shape[1]
    column = lax.broadcasted_iota(jnp.int32, value.shape, 1) % SIDE
    moved = pltpu.roll(value, cols % cells, 1)
    inside = column >= 1 if cols > 0 else column <= SIDE - 2
    return jnp.where(inside, moved, 0.0)


VMEM = pl.BlockSpec(memory_space=pltpu.VMEM)
PARAMS = pltpu.CompilerParams(vmem_limit_bytes=40 * 1024 * 1024)


def position():
    filt_at = lax.axis_index("filt")
    ring = lax.axis_size("filt") // 2
    return lax.axis_index("slab") % 2, filt_at % 2, filt_at % ring < ring // 2


def picked(rows, parity, block):
    channels = rows.shape[1]
    shape = (channels, channels // 2)
    source = lax.broadcasted_iota(jnp.int32, shape, 0)
    target = lax.broadcasted_iota(jnp.int32, shape, 1)
    side = target // block % 2
    member = target // (2 * block)
    base = side * (channels // 2) + 2 * member * block + target % block
    matrix = jnp.where(source == base + parity * block, 1.0, 0.0).astype(jnp.bfloat16)
    chosen = jnp.dot(rows, matrix, preferred_element_type=jnp.float32)
    return chosen.astype(jnp.bfloat16)


def pick_into(block, parity, weight_ref, own_ref, other_ref, buffer, sem):
    copy = pltpu.make_async_copy(weight_ref, buffer, sem)
    copy.start()
    copy.wait()
    taps, out_rows, channels = buffer.shape
    rows = buffer[...].reshape(taps * out_rows, channels)
    other_ref[...] = picked(rows, 1 - parity, block)
    own_ref[...] = picked(rows, parity, block)


def early_kernel(block, weight_ref, own_ref, send_ref, buffer, sem):
    _, parity, is_early = position()

    @pl.when(is_early)
    def _():
        pick_into(block, parity, weight_ref, own_ref, send_ref, buffer, sem)


def late_kernel(block, weight_ref, early_ref, received_ref, own_ref, other_ref, buffer, sem):
    _, parity, is_early = position()

    @pl.when(is_early)
    def _():
        own_ref[...] = early_ref[...]
        other_ref[...] = received_ref[...]

    @pl.when(jnp.logical_not(is_early))
    def _():
        pick_into(block, parity, weight_ref, own_ref, other_ref, buffer, sem)


def picks(body, block, weights, *early):
    taps, out_rows, channels = weights.shape
    out = jax.ShapeDtypeStruct((taps * out_rows, channels // 2), weights.dtype)
    slow = pl.CostEstimate(flops=10**10, bytes_accessed=0, transcendentals=0)
    return pl.pallas_call(
        functools.partial(body, block),
        out_shape=(out, out),
        in_specs=[pl.BlockSpec(memory_space=pltpu.HBM)] + [VMEM] * len(early),
        out_specs=(VMEM, VMEM),
        scratch_shapes=[pltpu.VMEM(weights.shape, weights.dtype), pltpu.SemaphoreType.DMA],
        compiler_params=PARAMS,
        cost_estimate=slow if early else None,
    )(pltpu.with_memory_space_constraint(weights, pltpu.HBM), *early)


def add_kernel(centre_ref, pair_ref, next_ref, own_ref, other_ref):
    odd, _, _ = position()
    out_rows = own_ref.shape[0]
    total = centre_ref[...] + pair_ref[1 - odd] + next_ref[...]
    other_ref[...] = total[out_rows:]
    own_ref[...] = total[:out_rows]


def added(centre, from_pair, from_next):
    half = jax.ShapeDtypeStruct((centre.shape[0] // 2, centre.shape[1]), centre.dtype)
    return pl.pallas_call(
        add_kernel,
        out_shape=(half, half),
        in_specs=[VMEM] * 3,
        out_specs=(VMEM,) * 2,
        compiler_params=PARAMS,
    )(centre, from_pair, from_next)


def in_plane(product):
    rows = product.shape[0] // 9
    taps = [product[tap * rows : (tap + 1) * rows] for tap in range(9)]
    by_col = [
        taps[3 + col] + shifted_rows(taps[col], 1) + shifted_rows(taps[6 + col], -1)
        for col in range(3)
    ]
    return by_col[1] + shifted_cols(by_col[0], 1) + shifted_cols(by_col[2], -1)


def plane_taps(plane, weight_ref, plane_off):
    rows = weight_ref.shape[0] // 3
    group = weight_ref[pl.ds(plane_off * rows, rows), :]
    return in_plane(jnp.dot(group, plane, preferred_element_type=jnp.float32))


def first_kernel(plane_ref, weight_ref, next_ref, pair_ref):
    plane = plane_ref[...]
    odd, _, _ = position()
    next_ref[...] = plane_taps(plane, weight_ref, 2 - 2 * odd)
    pair_ref[...] = plane_taps(plane, weight_ref, 2 * odd)


def second_kernel(plane_ref, weight_ref, first_next_ref, first_pair_ref, next_ref, pair_ref):
    plane = plane_ref[...]
    odd, _, _ = position()
    out_rows = first_next_ref.shape[0]
    next_ref[:out_rows] = first_next_ref[...]
    pair_ref[:out_rows] = first_pair_ref[...]
    next_ref[out_rows:] = plane_taps(plane, weight_ref, 2 - 2 * odd)
    pair_ref[out_rows:] = plane_taps(plane, weight_ref, 2 * odd)


def centre_kernel(plane_ref, second_ref, own_ref, other_ref, centre_ref):
    out_rows = centre_ref.shape[0] // 2
    centre_ref[:out_rows] = plane_taps(plane_ref[...], own_ref, 1)
    centre_ref[out_rows:] = plane_taps(second_ref[...], other_ref, 1)


def sums(body, out_rows, outs, *args):
    out = jax.ShapeDtypeStruct((out_rows, args[0].shape[1]), jnp.float32)
    return pl.pallas_call(
        body,
        out_shape=(out,) * outs,
        in_specs=[VMEM] * len(args),
        out_specs=(VMEM,) * outs,
        compiler_params=PARAMS,
    )(*args)


def on_device(volume, kernel, channel_bias):
    own_in, planes, cells = volume.shape
    own_out = kernel.shape[1]
    filt = lax.axis_size("filt")
    slabs = lax.axis_size("slab")
    ring = filt // 2
    rings = [[i, i + ring] for i in range(ring)]
    early = [i % ring < ring // 2 for i in range(filt)]
    swap_early = [(i, i ^ 1) for i in range(filt) if early[i]]
    swap_late = [(i, i ^ 1) for i in range(filt) if not early[i]]
    keep_early = [(i, i) for i in range(filt) if early[i]]
    keep_late = [(i, i) for i in range(filt) if not early[i]]
    alike = [
        list(range(half * ring + parity, (half + 1) * ring, 2))
        for half in range(2)
        for parity in range(2)
    ]
    pairs = [[i, i + 1] for i in range(0, slabs, 2)]
    nexts = [(i, i + 1) for i in range(1, slabs - 1, 2)]
    nexts += [(target, source) for source, target in nexts]
    early_own, for_partner = picks(early_kernel, own_in, kernel)
    received = lax.ppermute(for_partner, "filt", swap_early)
    block = volume.reshape(own_in, cells)
    both = lax.all_gather(block, "filt", axis=0, tiled=True, axis_index_groups=rings)
    plane = lax.all_gather(both, "filt", axis=0, tiled=True, axis_index_groups=alike)
    second = lax.ppermute(plane, "filt", keep_early + swap_late)
    own, other = picks(late_kernel, own_in, kernel, early_own, received)

    first = sums(first_kernel, own_out, 2, plane, own)
    to_next, to_pair = sums(second_kernel, 2 * own_out, 2, second, other, *first)
    from_next = lax.ppermute(to_next, "slab", nexts)
    from_pair = lax.all_gather(to_pair, "slab", axis=0, axis_index_groups=pairs)
    (centre,) = sums(centre_kernel, 2 * own_out, 1, plane, second, own, other)
    own_sum, other_sum = added(centre, from_pair, from_next)
    from_other = lax.ppermute(other_sum, "filt", swap_early + keep_late)
    summed = own_sum + from_other + channel_bias[:, None]
    return summed.reshape(own_out, planes, cells).astype(jnp.bfloat16)


def solution(mesh):
    return jax.shard_map(
        on_device,
        mesh=mesh,
        in_specs=(P("filt", "slab", None), P(None, "filt", None), P("filt")),
        out_specs=P("filt", "slab", None),
        check_vma=False,
    )
```

```python
import functools

import jax
import jax.numpy as jnp
from jax import lax
from jax.experimental import pallas as pl
from jax.experimental.pallas import tpu as pltpu
from jax.sharding import PartitionSpec as P

SIDE = 32


def shifted_rows(value, rows):
    cells = value.shape[1]
    place = lax.broadcasted_iota(jnp.int32, value.shape, 1)
    moved = pltpu.roll(value, (rows * SIDE) % cells, 1)
    inside = place >= rows * SIDE if rows > 0 else place < cells + rows * SIDE
    return jnp.where(inside, moved, 0.0)


def shifted_cols(value, cols):
    cells = value.shape[1]
    column = lax.broadcasted_iota(jnp.int32, value.shape, 1) % SIDE
    moved = pltpu.roll(value, cols % cells, 1)
    inside = column >= 1 if cols > 0 else column <= SIDE - 2
    return jnp.where(inside, moved, 0.0)


VMEM = pl.BlockSpec(memory_space=pltpu.VMEM)
PARAMS = pltpu.CompilerParams(vmem_limit_bytes=40 * 1024 * 1024)


def position():
    filt_at = lax.axis_index("filt")
    ring = lax.axis_size("filt") // 2
    return lax.axis_index("slab") % 2, filt_at % 2, filt_at % ring < ring // 2


def picked(rows, parity, block):
    channels = rows.shape[1]
    shape = (channels, channels // 2)
    source = lax.broadcasted_iota(jnp.int32, shape, 0)
    target = lax.broadcasted_iota(jnp.int32, shape, 1)
    side = target // block % 2
    member = target // (2 * block)
    base = side * (channels // 2) + 2 * member * block + target % block
    matrix = jnp.where(source == base + parity * block, 1.0, 0.0).astype(jnp.bfloat16)
    chosen = jnp.dot(rows, matrix, preferred_element_type=jnp.float32)
    return chosen.astype(jnp.bfloat16)


def pick_into(block, parity, weight_ref, own_ref, other_ref, buffer, sem):
    copy = pltpu.make_async_copy(weight_ref, buffer, sem)
    copy.start()
    copy.wait()
    taps, out_rows, channels = buffer.shape
    rows = buffer[...].reshape(taps * out_rows, channels)
    other_ref[...] = picked(rows, 1 - parity, block)
    own_ref[...] = picked(rows, parity, block)


def early_kernel(block, weight_ref, own_ref, send_ref, buffer, sem):
    _, parity, is_early = position()

    @pl.when(is_early)
    def _():
        pick_into(block, parity, weight_ref, own_ref, send_ref, buffer, sem)


def late_kernel(block, weight_ref, early_ref, received_ref, own_ref, other_ref, buffer, sem):
    _, parity, is_early = position()

    @pl.when(is_early)
    def _():
        own_ref[...] = early_ref[...]
        other_ref[...] = received_ref[...]

    @pl.when(jnp.logical_not(is_early))
    def _():
        pick_into(block, parity, weight_ref, own_ref, other_ref, buffer, sem)


def picks(body, block, weights, *early):
    taps, out_rows, channels = weights.shape
    out = jax.ShapeDtypeStruct((taps * out_rows, channels // 2), weights.dtype)
    slow = pl.CostEstimate(flops=10**10, bytes_accessed=0, transcendentals=0)
    return pl.pallas_call(
        functools.partial(body, block),
        out_shape=(out, out),
        in_specs=[pl.BlockSpec(memory_space=pltpu.HBM)] + [VMEM] * len(early),
        out_specs=(VMEM, VMEM),
        scratch_shapes=[pltpu.VMEM(weights.shape, weights.dtype), pltpu.SemaphoreType.DMA],
        compiler_params=PARAMS,
        cost_estimate=slow if early else None,
    )(pltpu.with_memory_space_constraint(weights, pltpu.HBM), *early)


def add_kernel(centre_ref, pair_ref, late_next_ref, early_next_ref, own_ref, other_ref):
    odd, _, _ = position()
    out_rows = own_ref.shape[0]
    total = centre_ref[...] + pair_ref[1 - odd] + early_next_ref[...]
    other_ref[...] = total[out_rows:]
    own_ref[...] = total[:out_rows] + late_next_ref[...]


def added(centre, *parts):
    half = jax.ShapeDtypeStruct((centre.shape[0] // 2, centre.shape[1]), centre.dtype)
    return pl.pallas_call(
        add_kernel,
        out_shape=(half, half),
        in_specs=[VMEM] * (1 + len(parts)),
        out_specs=(VMEM,) * 2,
        compiler_params=PARAMS,
    )(centre, *parts)


def in_plane(product):
    rows = product.shape[0] // 9
    taps = [product[tap * rows : (tap + 1) * rows] for tap in range(9)]
    by_col = [
        taps[3 + col] + shifted_rows(taps[col], 1) + shifted_rows(taps[6 + col], -1)
        for col in range(3)
    ]
    return by_col[1] + shifted_cols(by_col[0], 1) + shifted_cols(by_col[2], -1)


def plane_taps(plane, weight_ref, plane_off):
    rows = weight_ref.shape[0] // 3
    group = weight_ref[pl.ds(plane_off * rows, rows), :]
    return in_plane(jnp.dot(group, plane, preferred_element_type=jnp.float32))


def first_kernel(plane_ref, weight_ref, next_ref, pair_ref):
    plane = plane_ref[...]
    odd, _, _ = position()
    next_ref[...] = plane_taps(plane, weight_ref, 2 - 2 * odd)
    pair_ref[...] = plane_taps(plane, weight_ref, 2 * odd)


def shared(second):
    _, _, is_early = position()
    return jnp.where(is_early, jnp.zeros_like(second), second)


def second_kernel(
    plane_ref, weight_ref, first_next_ref, first_pair_ref, late_next_ref, early_next_ref, pair_ref
):
    plane = plane_ref[...]
    odd, _, _ = position()
    out_rows = first_next_ref.shape[0]
    away = plane_taps(plane, weight_ref, 2 - 2 * odd)
    late_next_ref[...] = first_next_ref[...] + away
    early_next_ref[:out_rows] = first_next_ref[...]
    early_next_ref[out_rows:] = away
    across = plane_taps(plane, weight_ref, 2 * odd)
    pair_ref[:out_rows] = first_pair_ref[...] + shared(across)
    pair_ref[out_rows:] = across


def centre_kernel(plane_ref, second_ref, own_ref, other_ref, centre_ref):
    out_rows = centre_ref.shape[0] // 2
    second = plane_taps(second_ref[...], other_ref, 1)
    centre_ref[:out_rows] = plane_taps(plane_ref[...], own_ref, 1) + shared(second)
    centre_ref[out_rows:] = second


def sums(body, out_rows, *args):
    cells = args[0].shape[1]
    return pl.pallas_call(
        body,
        out_shape=tuple(jax.ShapeDtypeStruct((rows, cells), jnp.float32) for rows in out_rows),
        in_specs=[VMEM] * len(args),
        out_specs=(VMEM,) * len(out_rows),
        compiler_params=PARAMS,
    )(*args)


def on_device(volume, kernel, channel_bias):
    own_in, planes, cells = volume.shape
    own_out = kernel.shape[1]
    filt = lax.axis_size("filt")
    slabs = lax.axis_size("slab")
    ring = filt // 2
    rings = [[i, i + ring] for i in range(ring)]
    early = [i % ring < ring // 2 for i in range(filt)]
    swap_early = [(i, i ^ 1) for i in range(filt) if early[i]]
    swap_late = [(i, i ^ 1) for i in range(filt) if not early[i]]
    keep_early = [(i, i) for i in range(filt) if early[i]]
    alike = [
        list(range(half * ring + parity, (half + 1) * ring, 2))
        for half in range(2)
        for parity in range(2)
    ]
    pairs = [[i, i + 1] for i in range(0, slabs, 2)]
    nexts = [(i, i + 1) for i in range(1, slabs - 1, 2)]
    nexts += [(target, source) for source, target in nexts]

    def crossing(members):
        return [
            (source * filt + i, target * filt + i)
            for source, target in nexts
            for i in range(filt)
            if members[i]
        ]

    early_own, for_partner = picks(early_kernel, own_in, kernel)
    received = lax.ppermute(for_partner, "filt", swap_early)
    block = volume.reshape(own_in, cells)
    both = lax.all_gather(block, "filt", axis=0, tiled=True, axis_index_groups=rings)
    plane = lax.all_gather(both, "filt", axis=0, tiled=True, axis_index_groups=alike)
    second = lax.ppermute(plane, "filt", keep_early + swap_late)
    own, other = picks(late_kernel, own_in, kernel, early_own, received)

    first = sums(first_kernel, (own_out, own_out), plane, own)
    late_to_next, early_to_next, to_pair = sums(
        second_kernel, (own_out, 2 * own_out, 2 * own_out), second, other, *first
    )
    both_axes = ("slab", "filt")
    early_from_next = lax.ppermute(early_to_next, both_axes, crossing(early))
    late_from_next = lax.ppermute(late_to_next, both_axes, crossing([not e for e in early]))
    from_pair = lax.all_gather(to_pair, "slab", axis=0, axis_index_groups=pairs)
    (centre,) = sums(centre_kernel, (2 * own_out,), plane, second, own, other)
    own_sum, other_sum = added(centre, from_pair, late_from_next, early_from_next)
    from_other = lax.ppermute(other_sum, "filt", swap_early)
    summed = own_sum + from_other + channel_bias[:, None]
    return summed.reshape(own_out, planes, cells).astype(jnp.bfloat16)


def solution(mesh):
    return jax.shard_map(
        on_device,
        mesh=mesh,
        in_specs=(P("filt", "slab", None), P(None, "filt", None), P("filt")),
        out_specs=P("filt", "slab", None),
        check_vma=False,
    )
```

```python
import functools

import jax
import jax.numpy as jnp
from jax import lax
from jax.experimental import pallas as pl
from jax.experimental.pallas import tpu as pltpu
from jax.sharding import PartitionSpec as P

SIDE = 32


def shifted_rows(value, rows):
    cells = value.shape[1]
    place = lax.broadcasted_iota(jnp.int32, (1, cells), 1)
    moved = pltpu.roll(value, (rows * SIDE) % cells, 1)
    inside = place >= rows * SIDE if rows > 0 else place < cells + rows * SIDE
    return jnp.where(inside, moved, 0.0)


def shifted_cols(value, cols):
    cells = value.shape[1]
    column = lax.broadcasted_iota(jnp.int32, (1, cells), 1) & (SIDE - 1)
    moved = pltpu.roll(value, cols % cells, 1)
    inside = column >= 1 if cols > 0 else column <= SIDE - 2
    return jnp.where(inside, moved, 0.0)


VMEM = pl.BlockSpec(memory_space=pltpu.VMEM)
PARAMS = pltpu.CompilerParams(vmem_limit_bytes=40 * 1024 * 1024)


def position():
    filt_at = lax.axis_index("filt")
    ring = lax.axis_size("filt") // 2
    return lax.axis_index("slab") % 2, filt_at % 2, filt_at % ring < ring // 2


def picked(rows, parity, block):
    channels = rows.shape[1]
    source = lax.broadcasted_iota(jnp.int32, (channels, channels // 2), 0)
    target = lax.broadcasted_iota(jnp.int32, (1, channels // 2), 1)
    side = target // block % 2
    member = target // (2 * block)
    wanted = side * (channels // 2) + (2 * member + parity) * block + target % block
    matrix = jnp.where(source == wanted, 1.0, 0.0).astype(jnp.bfloat16)
    chosen = jnp.dot(rows, matrix, preferred_element_type=jnp.float32)
    return chosen.astype(jnp.bfloat16)


def pick_into(block, parity, weight_ref, own_ref, other_ref, buffer, sem):
    copy = pltpu.make_async_copy(weight_ref, buffer, sem)
    copy.start()
    copy.wait()
    taps, out_rows, channels = buffer.shape
    rows = buffer[...].reshape(taps * out_rows, channels)
    other_ref[...] = picked(rows, 1 - parity, block)
    own_ref[...] = picked(rows, parity, block)


def early_kernel(block, weight_ref, own_ref, send_ref, buffer, sem):
    _, parity, is_early = position()

    @pl.when(is_early)
    def _():
        pick_into(block, parity, weight_ref, own_ref, send_ref, buffer, sem)


def late_kernel(block, weight_ref, early_ref, received_ref, own_ref, other_ref, buffer, sem):
    _, parity, is_early = position()

    @pl.when(is_early)
    def _():
        own_ref[...] = early_ref[...]
        other_ref[...] = received_ref[...]

    @pl.when(jnp.logical_not(is_early))
    def _():
        pick_into(block, parity, weight_ref, own_ref, other_ref, buffer, sem)


def picks(body, block, weights, *early):
    taps, out_rows, channels = weights.shape
    out = jax.ShapeDtypeStruct((taps * out_rows, channels // 2), weights.dtype)
    slow = pl.CostEstimate(flops=10**10, bytes_accessed=0, transcendentals=0)
    return pl.pallas_call(
        functools.partial(body, block),
        out_shape=(out, out),
        in_specs=[pl.BlockSpec(memory_space=pltpu.HBM)] + [VMEM] * len(early),
        out_specs=(VMEM, VMEM),
        scratch_shapes=[pltpu.VMEM(weights.shape, weights.dtype), pltpu.SemaphoreType.DMA],
        compiler_params=PARAMS,
        cost_estimate=slow if early else None,
    )(pltpu.with_memory_space_constraint(weights, pltpu.HBM), *early)


def add_kernel(centre_ref, late_next_ref, early_next_ref, own_ref, other_ref):
    out_rows = own_ref.shape[0]
    total = centre_ref[...] + early_next_ref[...]
    other_ref[...] = total[out_rows:]
    own_ref[...] = total[:out_rows] + late_next_ref[...]


def added(centre, *parts):
    half = jax.ShapeDtypeStruct((centre.shape[0] // 2, centre.shape[1]), centre.dtype)
    return pl.pallas_call(
        add_kernel,
        out_shape=(half, half),
        in_specs=[VMEM] * (1 + len(parts)),
        out_specs=(VMEM,) * 2,
        compiler_params=PARAMS,
    )(centre, *parts)


def in_plane(product):
    rows = product.shape[0] // 9
    taps = [product[tap * rows : (tap + 1) * rows] for tap in range(9)]
    by_col = [
        taps[3 + col] + shifted_rows(taps[col], 1) + shifted_rows(taps[6 + col], -1)
        for col in range(3)
    ]
    return by_col[1] + shifted_cols(by_col[0], 1) + shifted_cols(by_col[2], -1)


def plane_taps(plane, weight_ref, plane_off):
    rows = weight_ref.shape[0] // 3
    group = weight_ref[pl.ds(plane_off * rows, rows), :]
    return in_plane(jnp.dot(group, plane, preferred_element_type=jnp.float32))


def first_kernel(plane_ref, weight_ref, next_ref, pair_ref):
    plane = plane_ref[...]
    odd, _, _ = position()
    next_ref[...] = plane_taps(plane, weight_ref, 2 - 2 * odd)
    pair_ref[...] = plane_taps(plane, weight_ref, 2 * odd)


def shared(second):
    _, _, is_early = position()
    return jnp.where(is_early, jnp.zeros_like(second), second)


def away_kernel(plane_ref, weight_ref, first_ref, late_next_ref, early_next_ref):
    odd, _, _ = position()
    out_rows = first_ref.shape[0]
    second = plane_taps(plane_ref[...], weight_ref, 2 - 2 * odd)
    late_next_ref[...] = first_ref[...] + second
    early_next_ref[:out_rows] = first_ref[...]
    early_next_ref[out_rows:] = second


def across_kernel(plane_ref, weight_ref, first_ref, pair_ref):
    odd, _, _ = position()
    out_rows = first_ref.shape[0]
    second = plane_taps(plane_ref[...], weight_ref, 2 * odd)
    pair_ref[:out_rows] = first_ref[...] + shared(second)
    pair_ref[out_rows:] = second


def centre_kernel(plane_ref, second_ref, own_ref, other_ref, pair_ref, centre_ref):
    odd, _, _ = position()
    out_rows = centre_ref.shape[0] // 2
    pair = pair_ref[1 - odd]
    first = plane_taps(plane_ref[...], own_ref, 1)
    second = plane_taps(second_ref[...], other_ref, 1)
    centre_ref[:out_rows] = first + shared(second) + pair[:out_rows]
    centre_ref[out_rows:] = second + pair[out_rows:]


def sums(body, out_rows, *args):
    cells = args[0].shape[1]
    return pl.pallas_call(
        body,
        out_shape=tuple(jax.ShapeDtypeStruct((rows, cells), jnp.float32) for rows in out_rows),
        in_specs=[VMEM] * len(args),
        out_specs=(VMEM,) * len(out_rows),
        compiler_params=PARAMS,
    )(*args)


def on_device(volume, kernel, channel_bias):
    own_in, planes, cells = volume.shape
    own_out = kernel.shape[1]
    filt = lax.axis_size("filt")
    slabs = lax.axis_size("slab")
    ring = filt // 2
    rings = [[i, i + ring] for i in range(ring)]
    early = [i % ring < ring // 2 for i in range(filt)]
    swap_early = [(i, i ^ 1) for i in range(filt) if early[i]]
    swap_late = [(i, i ^ 1) for i in range(filt) if not early[i]]
    keep_early = [(i, i) for i in range(filt) if early[i]]
    alike = [
        list(range(half * ring + parity, (half + 1) * ring, 2))
        for half in range(2)
        for parity in range(2)
    ]
    pairs = [[i, i + 1] for i in range(0, slabs, 2)]
    nexts = [(i, i + 1) for i in range(1, slabs - 1, 2)]
    nexts += [(target, source) for source, target in nexts]

    def crossing(members):
        return [
            (source * filt + i, target * filt + i)
            for source, target in nexts
            for i in range(filt)
            if members[i]
        ]

    early_own, for_partner = picks(early_kernel, own_in, kernel)
    received = lax.ppermute(for_partner, "filt", swap_early)
    block = volume.reshape(own_in, cells)
    both = lax.all_gather(block, "filt", axis=0, tiled=True, axis_index_groups=rings)
    plane = lax.all_gather(both, "filt", axis=0, tiled=True, axis_index_groups=alike)
    second = lax.ppermute(plane, "filt", keep_early + swap_late)
    own, other = picks(late_kernel, own_in, kernel, early_own, received)

    first = sums(first_kernel, (own_out, own_out), plane, own)
    late_to_next, early_to_next = sums(
        away_kernel, (own_out, 2 * own_out), second, other, first[0]
    )
    (to_pair,) = sums(across_kernel, (2 * own_out,), second, other, first[1])
    both_axes = ("slab", "filt")
    early_from_next = lax.ppermute(early_to_next, both_axes, crossing(early))
    late_from_next = lax.ppermute(late_to_next, both_axes, crossing([not e for e in early]))
    from_pair = lax.all_gather(to_pair, "slab", axis=0, axis_index_groups=pairs)
    (centre,) = sums(centre_kernel, (2 * own_out,), plane, second, own, other, from_pair)
    own_sum, other_sum = added(centre, late_from_next, early_from_next)
    from_other = lax.ppermute(other_sum, "filt", swap_early)
    summed = own_sum + from_other + channel_bias[:, None]
    return summed.reshape(own_out, planes, cells).astype(jnp.bfloat16)


def solution(mesh):
    return jax.shard_map(
        on_device,
        mesh=mesh,
        in_specs=(P("filt", "slab", None), P(None, "filt", None), P("filt")),
        out_specs=P("filt", "slab", None),
        check_vma=False,
    )
```

```python
import functools

import jax
import jax.numpy as jnp
from jax import lax
from jax.experimental import pallas as pl
from jax.experimental.pallas import tpu as pltpu
from jax.sharding import PartitionSpec as P

SIDE = 32


def shifted_rows(value, rows):
    cells = value.shape[1]
    place = lax.broadcasted_iota(jnp.int32, (1, cells), 1)
    moved = pltpu.roll(value, (rows * SIDE) % cells, 1)
    inside = place >= rows * SIDE if rows > 0 else place < cells + rows * SIDE
    return jnp.where(inside, moved, 0.0)


def shifted_cols(value, cols):
    cells = value.shape[1]
    column = lax.broadcasted_iota(jnp.int32, (1, cells), 1) & (SIDE - 1)
    moved = pltpu.roll(value, cols % cells, 1)
    inside = column >= 1 if cols > 0 else column <= SIDE - 2
    return jnp.where(inside, moved, 0.0)


VMEM = pl.BlockSpec(memory_space=pltpu.VMEM)
PARAMS = pltpu.CompilerParams(vmem_limit_bytes=40 * 1024 * 1024)


def position():
    filt_at = lax.axis_index("filt")
    ring = lax.axis_size("filt") // 2
    return lax.axis_index("slab") % 2, filt_at % 2, filt_at % ring < ring // 2


def picked(rows, parity, block):
    channels = rows.shape[1]
    source = lax.broadcasted_iota(jnp.int32, (channels, channels // 2), 0)
    target = lax.broadcasted_iota(jnp.int32, (1, channels // 2), 1)
    side = target // block % 2
    member = target // (2 * block)
    wanted = side * (channels // 2) + (2 * member + parity) * block + target % block
    matrix = jnp.where(source == wanted, 1.0, 0.0).astype(jnp.bfloat16)
    chosen = jnp.dot(rows, matrix, preferred_element_type=jnp.float32)
    return chosen.astype(jnp.bfloat16)


def pick_into(block, parity, weight_ref, own_ref, other_ref, buffer, sem):
    copy = pltpu.make_async_copy(weight_ref, buffer, sem)
    copy.start()
    copy.wait()
    taps, out_rows, channels = buffer.shape
    rows = buffer[...].reshape(taps * out_rows, channels)
    other_ref[...] = picked(rows, 1 - parity, block)
    own_ref[...] = picked(rows, parity, block)


def early_kernel(block, weight_ref, own_ref, send_ref, buffer, sem):
    _, parity, is_early = position()

    @pl.when(is_early)
    def _():
        pick_into(block, parity, weight_ref, own_ref, send_ref, buffer, sem)


def late_kernel(block, weight_ref, early_ref, received_ref, own_ref, other_ref, buffer, sem):
    _, parity, is_early = position()

    @pl.when(is_early)
    def _():
        own_ref[...] = early_ref[...]
        other_ref[...] = received_ref[...]

    @pl.when(jnp.logical_not(is_early))
    def _():
        pick_into(block, parity, weight_ref, own_ref, other_ref, buffer, sem)


def picks(body, block, weights, *early):
    taps, out_rows, channels = weights.shape
    out = jax.ShapeDtypeStruct((taps * out_rows, channels // 2), weights.dtype)
    slow = pl.CostEstimate(flops=10**10, bytes_accessed=0, transcendentals=0)
    return pl.pallas_call(
        functools.partial(body, block),
        out_shape=(out, out),
        in_specs=[pl.BlockSpec(memory_space=pltpu.HBM)] + [VMEM] * len(early),
        out_specs=(VMEM, VMEM),
        scratch_shapes=[pltpu.VMEM(weights.shape, weights.dtype), pltpu.SemaphoreType.DMA],
        compiler_params=PARAMS,
        cost_estimate=slow if early else None,
    )(pltpu.with_memory_space_constraint(weights, pltpu.HBM), *early)


def add_kernel(centre_ref, early_next_ref, own_ref, other_ref):
    out_rows = own_ref.shape[0]
    other_ref[...] = centre_ref[out_rows:] + early_next_ref[out_rows:]
    own_ref[...] = centre_ref[:out_rows] + early_next_ref[:out_rows]


def added(centre, early_next):
    half = jax.ShapeDtypeStruct((centre.shape[0] // 2, centre.shape[1]), centre.dtype)
    return pl.pallas_call(
        add_kernel,
        out_shape=(half, half),
        in_specs=[VMEM] * 2,
        out_specs=(VMEM,) * 2,
        compiler_params=PARAMS,
    )(centre, early_next)


def in_plane(product):
    rows = product.shape[0] // 9
    taps = [product[tap * rows : (tap + 1) * rows] for tap in range(9)]
    by_col = [
        taps[3 + col] + shifted_rows(taps[col], 1) + shifted_rows(taps[6 + col], -1)
        for col in range(3)
    ]
    return by_col[1] + shifted_cols(by_col[0], 1) + shifted_cols(by_col[2], -1)


def plane_taps(plane, weight_ref, plane_off):
    rows = weight_ref.shape[0] // 3
    group = weight_ref[pl.ds(plane_off * rows, rows), :]
    return in_plane(jnp.dot(group, plane, preferred_element_type=jnp.float32))


def first_kernel(plane_ref, weight_ref, next_ref):
    odd, _, _ = position()
    next_ref[...] = plane_taps(plane_ref[...], weight_ref, 2 - 2 * odd)


def shared(second):
    _, _, is_early = position()
    return jnp.where(is_early, jnp.zeros_like(second), second)


def away_kernel(plane_ref, weight_ref, first_ref, late_next_ref, early_next_ref):
    odd, _, _ = position()
    out_rows = first_ref.shape[0]
    second = plane_taps(plane_ref[...], weight_ref, 2 - 2 * odd)
    late_next_ref[...] = first_ref[...] + second
    early_next_ref[:out_rows] = first_ref[...]
    early_next_ref[out_rows:] = second


def across_kernel(plane_ref, second_ref, own_ref, other_ref, pair_ref):
    odd, _, _ = position()
    out_rows = pair_ref.shape[0] // 2
    second = plane_taps(second_ref[...], other_ref, 2 * odd)
    pair_ref[:out_rows] = plane_taps(plane_ref[...], own_ref, 2 * odd) + shared(second)
    pair_ref[out_rows:] = second


def centre_kernel(plane_ref, second_ref, own_ref, other_ref, pair_ref, centre_ref):
    odd, _, _ = position()
    out_rows = centre_ref.shape[0] // 2
    pair = pair_ref[1 - odd]
    first = plane_taps(plane_ref[...], own_ref, 1)
    second = plane_taps(second_ref[...], other_ref, 1)
    centre_ref[:out_rows] = first + shared(second) + pair[:out_rows]
    centre_ref[out_rows:] = second + pair[out_rows:]


def sums(body, out_rows, *args):
    cells = args[0].shape[1]
    return pl.pallas_call(
        body,
        out_shape=tuple(jax.ShapeDtypeStruct((rows, cells), jnp.float32) for rows in out_rows),
        in_specs=[VMEM] * len(args),
        out_specs=(VMEM,) * len(out_rows),
        compiler_params=PARAMS,
    )(*args)


def on_device(volume, kernel, channel_bias):
    own_in, planes, cells = volume.shape
    own_out = kernel.shape[1]
    filt = lax.axis_size("filt")
    slabs = lax.axis_size("slab")
    ring = filt // 2
    rings = [[i, i + ring] for i in range(ring)]
    early = [i % ring < ring // 2 for i in range(filt)]
    swap_early = [(i, i ^ 1) for i in range(filt) if early[i]]
    swap_late = [(i, i ^ 1) for i in range(filt) if not early[i]]
    keep_early = [(i, i) for i in range(filt) if early[i]]
    alike = [
        list(range(half * ring + parity, (half + 1) * ring, 2))
        for half in range(2)
        for parity in range(2)
    ]
    pairs = [[i, i + 1] for i in range(0, slabs, 2)]
    nexts = [(i, i + 1) for i in range(1, slabs - 1, 2)]
    nexts += [(target, source) for source, target in nexts]

    def crossing(members):
        return [
            (source * filt + i, target * filt + i)
            for source, target in nexts
            for i in range(filt)
            if members[i]
        ]

    early_own, for_partner = picks(early_kernel, own_in, kernel)
    received = lax.ppermute(for_partner, "filt", swap_early)
    block = volume.reshape(own_in, cells)
    both = lax.all_gather(block, "filt", axis=0, tiled=True, axis_index_groups=rings)
    plane = lax.all_gather(both, "filt", axis=0, tiled=True, axis_index_groups=alike)
    second = lax.ppermute(plane, "filt", keep_early + swap_late)
    own, other = picks(late_kernel, own_in, kernel, early_own, received)

    (first,) = sums(first_kernel, (own_out,), plane, own)
    late_to_next, early_to_next = sums(
        away_kernel, (own_out, 2 * own_out), second, other, first
    )
    (to_pair,) = sums(across_kernel, (2 * own_out,), plane, second, own, other)
    both_axes = ("slab", "filt")
    early_from_next = lax.ppermute(early_to_next, both_axes, crossing(early))
    late_from_next = lax.ppermute(late_to_next, both_axes, crossing([not e for e in early]))
    from_pair = lax.all_gather(to_pair, "slab", axis=0, axis_index_groups=pairs)
    (centre,) = sums(centre_kernel, (2 * own_out,), plane, second, own, other, from_pair)
    own_sum, other_sum = added(centre, early_from_next)
    from_other = lax.ppermute(other_sum, "filt", swap_early)
    summed = own_sum + late_from_next + from_other + channel_bias[:, None]
    return summed.reshape(own_out, planes, cells).astype(jnp.bfloat16)


def solution(mesh):
    return jax.shard_map(
        on_device,
        mesh=mesh,
        in_specs=(P("filt", "slab", None), P(None, "filt", None), P("filt")),
        out_specs=P("filt", "slab", None),
        check_vma=False,
    )
```

```python
import functools

import jax
import jax.numpy as jnp
from jax import lax
from jax.experimental import pallas as pl
from jax.experimental.pallas import tpu as pltpu
from jax.sharding import PartitionSpec as P

SIDE = 32


def shifted_rows(value, rows):
    cells = value.shape[1]
    place = lax.broadcasted_iota(jnp.int32, (1, cells), 1)
    moved = pltpu.roll(value, (rows * SIDE) % cells, 1)
    inside = place >= rows * SIDE if rows > 0 else place < cells + rows * SIDE
    return jnp.where(inside, moved, 0.0)


def shifted_cols(value, cols):
    cells = value.shape[1]
    column = lax.broadcasted_iota(jnp.int32, (1, cells), 1) & (SIDE - 1)
    moved = pltpu.roll(value, cols % cells, 1)
    inside = column >= 1 if cols > 0 else column <= SIDE - 2
    return jnp.where(inside, moved, 0.0)


VMEM = pl.BlockSpec(memory_space=pltpu.VMEM)
PARAMS = pltpu.CompilerParams(vmem_limit_bytes=40 * 1024 * 1024)


def position():
    filt_at = lax.axis_index("filt")
    ring = lax.axis_size("filt") // 2
    return lax.axis_index("slab") % 2, filt_at % 2, filt_at % ring < ring // 2


def picked(rows, parity, block):
    channels = rows.shape[1]
    source = lax.broadcasted_iota(jnp.int32, (channels, channels // 2), 0)
    target = lax.broadcasted_iota(jnp.int32, (1, channels // 2), 1)
    side = target // block % 2
    member = target // (2 * block)
    wanted = side * (channels // 2) + (2 * member + parity) * block + target % block
    matrix = jnp.where(source == wanted, 1.0, 0.0).astype(jnp.bfloat16)
    chosen = jnp.dot(rows, matrix, preferred_element_type=jnp.float32)
    return chosen.astype(jnp.bfloat16)


def pick_into(block, parity, weight_ref, own_ref, other_ref, buffer, sem):
    copy = pltpu.make_async_copy(weight_ref, buffer, sem)
    copy.start()
    copy.wait()
    taps, out_rows, channels = buffer.shape
    rows = buffer[...].reshape(taps * out_rows, channels)
    other_ref[...] = picked(rows, 1 - parity, block)
    own_ref[...] = picked(rows, parity, block)


def early_kernel(block, weight_ref, own_ref, send_ref, buffer, sem):
    _, parity, is_early = position()

    @pl.when(is_early)
    def _():
        pick_into(block, parity, weight_ref, own_ref, send_ref, buffer, sem)


def late_kernel(block, weight_ref, early_ref, received_ref, own_ref, other_ref, buffer, sem):
    _, parity, is_early = position()

    @pl.when(is_early)
    def _():
        own_ref[...] = early_ref[...]
        other_ref[...] = received_ref[...]

    @pl.when(jnp.logical_not(is_early))
    def _():
        pick_into(block, parity, weight_ref, own_ref, other_ref, buffer, sem)


def picks(body, block, weights, *early):
    taps, out_rows, channels = weights.shape
    out = jax.ShapeDtypeStruct((taps * out_rows, channels // 2), weights.dtype)
    slow = pl.CostEstimate(flops=10**10, bytes_accessed=0, transcendentals=0)
    return pl.pallas_call(
        functools.partial(body, block),
        out_shape=(out, out),
        in_specs=[pl.BlockSpec(memory_space=pltpu.HBM)] + [VMEM] * len(early),
        out_specs=(VMEM, VMEM),
        scratch_shapes=[pltpu.VMEM(weights.shape, weights.dtype), pltpu.SemaphoreType.DMA],
        compiler_params=PARAMS,
        cost_estimate=slow if early else None,
    )(pltpu.with_memory_space_constraint(weights, pltpu.HBM), *early)


def in_plane(product):
    rows = product.shape[0] // 9
    taps = [product[tap * rows : (tap + 1) * rows] for tap in range(9)]
    by_col = [
        taps[3 + col] + shifted_rows(taps[col], 1) + shifted_rows(taps[6 + col], -1)
        for col in range(3)
    ]
    return by_col[1] + shifted_cols(by_col[0], 1) + shifted_cols(by_col[2], -1)


def plane_taps(plane, weight_ref, plane_off):
    rows = weight_ref.shape[0] // 3
    group = weight_ref[pl.ds(plane_off * rows, rows), :]
    return in_plane(jnp.dot(group, plane, preferred_element_type=jnp.float32))


def first_kernel(plane_ref, weight_ref, next_ref):
    odd, _, _ = position()
    next_ref[...] = plane_taps(plane_ref[...], weight_ref, 2 - 2 * odd)


def shared(second):
    _, _, is_early = position()
    return jnp.where(is_early, jnp.zeros_like(second), second)


def away_kernel(plane_ref, weight_ref, first_ref, late_next_ref, early_next_ref):
    odd, _, _ = position()
    out_rows = first_ref.shape[0]
    second = plane_taps(plane_ref[...], weight_ref, 2 - 2 * odd)
    late_next_ref[...] = first_ref[...] + second
    early_next_ref[:out_rows] = first_ref[...]
    early_next_ref[out_rows:] = second


def across_kernel(plane_ref, second_ref, own_ref, other_ref, pair_ref):
    odd, _, _ = position()
    out_rows = pair_ref.shape[0] // 2
    second = plane_taps(second_ref[...], other_ref, 2 * odd)
    pair_ref[:out_rows] = plane_taps(plane_ref[...], own_ref, 2 * odd) + shared(second)
    pair_ref[out_rows:] = second


def other_add_kernel(first_ref, next_ref, sum_ref):
    sum_ref[...] = first_ref[...] + next_ref[first_ref.shape[0] :]


def other_centre_kernel(second_ref, weight_ref, pair_ref, centre_ref, sum_ref):
    odd, _, _ = position()
    out_rows = sum_ref.shape[0]
    centre = plane_taps(second_ref[...], weight_ref, 1)
    centre_ref[...] = centre
    sum_ref[...] = centre + pair_ref[1 - odd, out_rows:]


def own_centre_kernel(plane_ref, weight_ref, pair_ref, next_ref, second_ref, sum_ref):
    odd, _, _ = position()
    out_rows = sum_ref.shape[0]
    centre = plane_taps(plane_ref[...], weight_ref, 1) + shared(second_ref[...])
    sum_ref[...] = centre + pair_ref[1 - odd, :out_rows] + next_ref[:out_rows]


def sums(body, out_rows, *args):
    cells = args[0].shape[1]
    return pl.pallas_call(
        body,
        out_shape=tuple(jax.ShapeDtypeStruct((rows, cells), jnp.float32) for rows in out_rows),
        in_specs=[VMEM] * len(args),
        out_specs=(VMEM,) * len(out_rows),
        compiler_params=PARAMS,
    )(*args)


def on_device(volume, kernel, channel_bias):
    own_in, planes, cells = volume.shape
    own_out = kernel.shape[1]
    filt = lax.axis_size("filt")
    slabs = lax.axis_size("slab")
    ring = filt // 2
    rings = [[i, i + ring] for i in range(ring)]
    early = [i % ring < ring // 2 for i in range(filt)]
    swap_early = [(i, i ^ 1) for i in range(filt) if early[i]]
    swap_late = [(i, i ^ 1) for i in range(filt) if not early[i]]
    keep_early = [(i, i) for i in range(filt) if early[i]]
    alike = [
        list(range(half * ring + parity, (half + 1) * ring, 2))
        for half in range(2)
        for parity in range(2)
    ]
    pairs = [[i, i + 1] for i in range(0, slabs, 2)]
    nexts = [(i, i + 1) for i in range(1, slabs - 1, 2)]
    nexts += [(target, source) for source, target in nexts]

    def crossing(members):
        return [
            (source * filt + i, target * filt + i)
            for source, target in nexts
            for i in range(filt)
            if members[i]
        ]

    early_own, for_partner = picks(early_kernel, own_in, kernel)
    received = lax.ppermute(for_partner, "filt", swap_early)
    block = volume.reshape(own_in, cells)
    both = lax.all_gather(block, "filt", axis=0, tiled=True, axis_index_groups=rings)
    plane = lax.all_gather(both, "filt", axis=0, tiled=True, axis_index_groups=alike)
    second = lax.ppermute(plane, "filt", keep_early + swap_late)
    own, other = picks(late_kernel, own_in, kernel, early_own, received)

    (first,) = sums(first_kernel, (own_out,), plane, own)
    late_to_next, early_to_next = sums(
        away_kernel, (own_out, 2 * own_out), second, other, first
    )
    (to_pair,) = sums(across_kernel, (2 * own_out,), plane, second, own, other)
    both_axes = ("slab", "filt")
    early_from_next = lax.ppermute(early_to_next, both_axes, crossing(early))
    late_from_next = lax.ppermute(late_to_next, both_axes, crossing([not e for e in early]))
    from_pair = lax.all_gather(to_pair, "slab", axis=0, axis_index_groups=pairs)
    halo = (from_pair, early_from_next)
    centre, other_sum = sums(
        other_centre_kernel, (own_out, own_out), second, other, from_pair
    )
    (other_sum,) = sums(other_add_kernel, (own_out,), other_sum, early_from_next)
    from_other = lax.ppermute(other_sum, "filt", swap_early)
    (own_sum,) = sums(own_centre_kernel, (own_out,), plane, own, *halo, centre)
    summed = own_sum + late_from_next + from_other + channel_bias[:, None]
    return summed.reshape(own_out, planes, cells).astype(jnp.bfloat16)


def solution(mesh):
    return jax.shard_map(
        on_device,
        mesh=mesh,
        in_specs=(P("filt", "slab", None), P(None, "filt", None), P("filt")),
        out_specs=P("filt", "slab", None),
        check_vma=False,
    )
```
